256 devices in a mesh: section: 2 (over z_hi), dp: 16 (over z_lo, x), seq: 8 (over y, core).
Axes of the slice: x: 4, y: 4, z: 8 (z_hi: 2, z_lo: 4; z = z_hi * 4 + z_lo), core: 2. Of those that a mesh axis runs over, the one named last changes fastest.
Arguments:
- qkv_rows: bfloat16 [2, 16, 1024, 9216], P('section', 'dp', 'seq'), may hold values from -30 to 30
- gate: float32 [2, 16, 3072], P('section', 'dp'), may hold values from -4 to 4
- out_weight: bfloat16 [3072, 3072], P('seq'), may hold values from -0.109375 to 0.109375
- out_grad: bfloat16 [2, 16, 1024, 3072], P('section', 'dp', 'seq'), may hold values from -6 to 6
- tile_order: int32 [1024], replicated, may hold values from 0 to 1023, as said below
- window: int32 [16, 6], replicated, may hold values from 0 to 15, as said below
Outputs:
- gated_out: bfloat16 [2, 16, 1024, 3072], P('section', 'dp', 'seq')
- weight_grad: float32 [3072, 3072], P('seq', ('section', 'dp'))
- gate_grad: float32 [2, 16, 3072], P('section', 'dp')
The draws below stay inside these ranges and needn't reach their ends.
Inputs may be any that keep to these rules, and one draw needn't show every extreme that they name: `tile_order`: lists every token once. `window`: row t names 6 different tiles, the first of them t itself.
All inputs are finite; a program needn't handle non-finite values.
Results may differ from the reference program's by a relative error of at most 0.023.
Values may be sent and summed in bfloat16 or wider, within the bound.
A program may use at most 128 MiB of HBM per device.

```python
import math
import jax
import jax.numpy as jnp
from jax import lax

D = 3072
HEADS = 24
TILE = 64
KT = 6
HEAD_DIM = 128
TOKENS = 1024
NTILES = 16
N_SECTION = 2
N_DP = 16
N_SEQ = 8


def shuffled_slots(key):
    return jax.random.permutation(jax.random.fold_in(key, 11), TOKENS).astype(jnp.int32)


def draw_tile_order(key, part):
    return shuffled_slots(key)


def draw_window(key, part):
    row_keys = jax.random.split(jax.random.fold_in(key, 23), NTILES)

    def row_shuffle(row_key):
        return jax.random.permutation(row_key, NTILES - 1).astype(jnp.int32)
    others = jax.vmap(row_shuffle)(row_keys) + 1
    offsets = jnp.concatenate([jnp.zeros((NTILES, 1), jnp.int32), others[:, :KT - 1]], axis=1)
    tile_ids = jnp.arange(NTILES, dtype=jnp.int32)
    return ((tile_ids[:, None] + offsets) % NTILES).astype(jnp.int32)


def draw_qkv_rows(key, part):
    full_shape = (N_SECTION, N_DP, TOKENS, 3, HEADS, HEAD_DIM)
    noise_key = jax.random.fold_in(key, 31)
    values = jnp.clip(jax.random.normal(noise_key, full_shape, jnp.float32), -6.0, 6.0)
    return values.reshape(N_SECTION, N_DP, TOKENS, 3 * D).astype(jnp.bfloat16)


def strengthened(array, stream_key, source, target, blocks, factor):
    def block_of(axis_at):
        return (jnp.arange(array.shape[axis_at]) // (array.shape[axis_at] // blocks)).reshape((-1,) + (1,) * (array.ndim - 1 - axis_at))

    near = jax.random.permutation(stream_key, blocks)[block_of(target)]
    far = (block_of(target) + blocks // 2) % blocks
    return jnp.where((block_of(source) == near) | (block_of(source) == far), factor * array, array)


def shard_levels(own_key, dims, cuts, low, largest):
    level = 1.0
    for position, shards_of in cuts:
        draws = jax.random.uniform(jax.random.fold_in(jax.random.fold_in(own_key, 6), position), (shards_of,), jnp.float32, low / len(cuts), largest / len(cuts))
        level = level * jnp.repeat(jnp.exp(draws), dims[position] // shards_of).reshape((-1,) + (1,) * (len(dims) - 1 - position))
    return level


def centred(key, dims, spread, most, cuts=(), kind=jnp.bfloat16):
    loudness = shard_levels(key, dims, cuts, -0.22, 0.18) if cuts else 1.0
    result = jax.random.normal(key, dims, jnp.float32) * spread * loudness
    return jnp.minimum(jnp.maximum(result, -most), most).astype(kind)


def bell_draw_with(key, shape, scale, most, shards, heavy, kind=jnp.bfloat16):
    entries = scale * jax.random.normal(key, shape, jnp.float32)
    if shards:
        entries = entries * shard_levels(key, shape, shards, -0.22, 0.18)
    return jnp.clip(strengthened(entries, jax.random.fold_in(key, 3), *heavy), -most, most).astype(kind)


def setup_inputs(seed: int = 0) -> dict:
    streams_of = jax.random.split(jax.random.key(seed), 7)
    qkv_rows = draw_qkv_rows(jax.random.fold_in(streams_of[6], 71), 0)
    gate = centred(streams_of[1], (N_SECTION, N_DP, D), 1.0, 4.0, ((0, 2), (1, 16)), jnp.float32)
    out_weight = centred(streams_of[2], (D, D), D ** -0.5, 0.109375, ((0, 8),))
    out_grad = bell_draw_with(streams_of[3], (N_SECTION, N_DP, TOKENS, D), 1.0, 6.0, ((0, 2), (1, 16), (2, 8)), (1, 3, 16, 2.0))
    tile_order = draw_tile_order(jax.random.fold_in(streams_of[6], 71), 0)
    window = draw_window(jax.random.fold_in(streams_of[6], 71), 0)
    return dict(qkv_rows=qkv_rows, gate=gate, out_weight=out_weight, out_grad=out_grad, tile_order=tile_order, window=window)


def attend_heads(source, tile_order, window):
    head_count = source.shape[2]
    tiled_rows = source[tile_order].reshape(NTILES, TILE, 3, head_count, HEAD_DIM)
    scale_factor = 1.0 / math.sqrt(HEAD_DIM)

    def one_tile(tile_index):
        queries = tiled_rows[tile_index, :, 0].astype(jnp.float32)
        gathered = tiled_rows[window[tile_index]].reshape(KT * TILE, 3, head_count, HEAD_DIM)
        key_rows = gathered[:, 1].astype(jnp.float32)
        value_rows = gathered[:, 2].astype(jnp.float32)
        scores = jnp.einsum('qhd,khd->hqk', queries, key_rows, precision=lax.Precision.HIGHEST) * scale_factor
        weights = jax.nn.softmax(scores, axis=-1).astype(jnp.bfloat16)
        mixed_rows = jnp.einsum('hqk,khd->qhd', weights.astype(jnp.float32), value_rows, precision=lax.Precision.HIGHEST)
        return mixed_rows.astype(jnp.bfloat16)
    tiles_out = lax.map(one_tile, jnp.arange(NTILES, dtype=jnp.int32), batch_size=8)
    flat_rows = tiles_out.reshape(TOKENS, head_count * HEAD_DIM)
    return jnp.zeros_like(flat_rows).at[tile_order].set(flat_rows)

def reference(qkv_rows, gate, out_weight, out_grad, tile_order, window):
    shifted = jnp.roll(qkv_rows, 1, axis=0)
    flat_source = shifted.reshape(N_SECTION * N_DP, TOKENS, 3, HEADS, HEAD_DIM)
    flat_gate = gate.reshape(N_SECTION * N_DP, D)
    flat_grad = out_grad.reshape(N_SECTION * N_DP, TOKENS, D)
    grouped_weight = out_weight.reshape(N_SEQ, D // N_SEQ, D).astype(jnp.float32)

    def per_sample(running, inputs):
        source, gate_row, grad_rows = inputs
        attended = attend_heads(source, tile_order, window)
        grouped = attended.reshape(TOKENS, N_SEQ, D // N_SEQ).astype(jnp.float32)
        partial_terms = jnp.einsum('tgf,gfo->gto', grouped, grouped_weight, precision=lax.Precision.HIGHEST).astype(jnp.bfloat16)
        partial_terms = lax.optimization_barrier(partial_terms)
        projected = lax.optimization_barrier(jnp.sum(partial_terms.astype(jnp.float32), axis=0))
        gated_rows = (gate_row * projected).astype(jnp.bfloat16)
        grad_float = grad_rows.astype(jnp.float32)
        gate_term = lax.optimization_barrier(jnp.sum(grad_float * projected, axis=0))
        proj_grad = (gate_row * grad_float).astype(jnp.bfloat16)
        update = jnp.dot(attended.T, proj_grad, preferred_element_type=jnp.float32)
        return (running + update, (gated_rows, gate_term))
    zero_grad = jnp.zeros((D, D), jnp.float32)
    weight_grad, (gated_out, gate_grad) = lax.scan(per_sample, zero_grad, (flat_source, flat_gate, flat_grad))
    return (gated_out.reshape(N_SECTION, N_DP, TOKENS, D), weight_grad, gate_grad.reshape(N_SECTION, N_DP, D))
```

```python
import functools
import math

import jax
import jax.numpy as jnp
from jax import lax
from jax.experimental import pallas as pl
from jax.experimental.pallas import tpu as pltpu
from jax.sharding import PartitionSpec as P

MESH = pl.DeviceIdType.MESH
TILE = 64
HEAD = 128
BF = jnp.bfloat16
F32 = jnp.float32
MASKED = -(2.0**30)
NY, NX, NZ, NQ = 4, 4, 8, 8
HEADS_HERE = 3


def kernel(
    qkv, gate, weight, grad, order, window,
    gated_out, wgrad_out, ggrad_out,
    qkv_v, qx, kx, att_v, att_r, w_v, grad_v, pg, part, rs_s, rs_r, gg,
    own, ex_s, ex_r, zs, zr, xs, xr, xown,
    local_sem, a2a_s, a2a_r, swap_s, swap_r, w_s, w_r, ag_s, ag_r, y_s, y_r,
    gg_s, gg_r, ex_ss, ex_rs, z_s, z_r, x_s, x_r,
):
    sec, dp, q = lax.axis_index("section"), lax.axis_index("dp"), lax.axis_index("seq")
    zl, x = dp // NX, dp % NX
    y, c = q // 2, q % 2
    z = sec * (NZ // 2) + zl
    rows = qkv.shape[0]
    width = grad.shape[1]
    feats = HEADS_HERE * HEAD

    def at_seq(j):
        return {"seq": j}

    def at_y(dy):
        return {"seq": ((y + dy) % NY) * 2 + c}

    def at_z(dz):
        there = (z + dz) % NZ
        return {"section": there // (NZ // 2), "dp": (there % (NZ // 2)) * NX + x}

    def at_x(dx):
        return {"dp": zl * NX + (x + dx) % NX}

    def opposite(core):
        return {"section": 1 - sec, "seq": y * 2 + core}

    other = {"seq": y * 2 + 1 - c}

    def send(src, dst, s_sem, r_sem, where):
        copy = pltpu.make_async_remote_copy(
            src_ref=src, dst_ref=dst, send_sem=s_sem, recv_sem=r_sem, device_id=where, device_id_type=MESH
        )
        copy.start()

    def landed(ref, sem):
        pltpu.make_async_copy(ref, ref, sem).wait()

    barrier = pltpu.get_barrier_semaphore()
    partners = [at_seq((q + k) % NQ) for k in range(1, NQ)]
    partners += [opposite(0), opposite(1), at_z(1), at_z(NZ - 1)]
    partners += [at_x(k) for k in range(1, NX)]
    for partner in partners:
        pl.semaphore_signal(barrier, inc=1, device_id=partner, device_id_type=MESH)
    pl.semaphore_wait(barrier, len(partners))

    mine = pl.ds(pl.multiple_of(q * rows, rows), rows)
    for head in range(HEADS_HERE):
        for what in range(3):

            def columns(j):
                return pl.ds(pl.multiple_of(what * width + j * feats + head * HEAD, HEAD), HEAD)

            def one_peer(k, carry):
                j = (q + k) % NQ
                send(
                    qkv.at[:, columns(j)], qkv_v.at[head, what, mine, :], a2a_s, a2a_r.at[head], at_seq(j)
                )
                return carry

            lax.fori_loop(1, NQ, one_peer, 0)
            pltpu.make_async_copy(
                qkv.at[:, columns(q)], qkv_v.at[head, what, mine, :], local_sem.at[head]
            ).start()

    send(weight, w_v.at[pl.ds(feats, feats), :], w_s, w_r, other)
    pltpu.make_async_copy(weight, w_v.at[pl.ds(0, feats), :], local_sem.at[3]).start()
    pltpu.make_async_copy(grad, grad_v, local_sem.at[4]).start()

    slot_tile = lax.broadcasted_iota(jnp.int32, (NQ * rows, HEAD), 0) >> 6
    in_tile = jnp.where(slot_tile == lax.broadcasted_iota(jnp.int32, (NQ * rows, HEAD), 1), 1.0, 0.0).astype(BF)
    tiles = window.shape[0]
    tile_ids = lax.broadcasted_iota(jnp.int32, (tiles, HEAD), 1)
    chosen = tile_ids == window[:, 0:1]
    for k in range(1, window.shape[1]):
        chosen = jnp.logical_or(chosen, tile_ids == window[:, k : k + 1])
    bias = jnp.where(chosen, 0.0, MASKED)
    bias = jnp.concatenate([bias, jnp.zeros((HEAD - tiles, HEAD), F32)], axis=0).astype(BF)
    for part_of in range(NY):
        here = pl.ds(part_of * 2 * rows, 2 * rows)
        tokens = lax.broadcasted_iota(jnp.int32, (2 * rows, NQ * rows), 0) + part_of * 2 * rows
        placed = jnp.where(tokens == order[...], 1.0, 0.0).astype(BF)
        tile_of = jnp.dot(placed, in_tile, preferred_element_type=F32).astype(BF)
        kx[here, :] = tile_of
        qx[here, :] = jnp.dot(tile_of, bias, preferred_element_type=F32).astype(BF)

    pltpu.make_async_copy(grad, grad_v, local_sem.at[4]).wait()
    pg[y] = (gate[...] * grad_v[...].astype(F32)).astype(BF)

    scale = 1.0 / math.sqrt(HEAD)
    for head in range(HEADS_HERE):
        landed(qkv_v.at[head, :, pl.ds(0, (NQ - 1) * rows), :], a2a_r.at[head])
        landed(qkv_v.at[head, :, pl.ds(0, rows), :], local_sem.at[head])
        if head == HEADS_HERE - 1:
            send(pg.at[y], pg.at[y], ag_s.at[0], ag_r.at[0], at_y(1))
            send(pg.at[y], pg.at[y], ag_s.at[1], ag_r.at[1], at_y(NY - 1))

        def attend(chunk, carry):
            here = pl.ds(pl.multiple_of(chunk * 2 * rows, 2 * rows), 2 * rows)
            queries = jnp.concatenate([qkv_v[head, 0, here, :], qx[here, :]], axis=1)
            keys = jnp.concatenate([qkv_v[head, 1], kx[...]], axis=1)
            scores = lax.dot_general(
                queries, keys, (((1,), (1,)), ((), ())), preferred_element_type=F32
            )
            top = jnp.max(scores, axis=1, keepdims=True)
            powers = jnp.exp((scores - top) * scale)
            total = jnp.sum(powers, axis=1, keepdims=True)
            mixed = jnp.dot(powers.astype(BF), qkv_v[head, 2], preferred_element_type=F32) / total
            att_v[head, chunk] = mixed.astype(BF).reshape(2, rows, HEAD)
            send(
                att_v.at[head, chunk, c],
                att_r.at[chunk, :, pl.ds(head * HEAD, HEAD)],
                swap_s, swap_r.at[head], opposite(c),
            )
            send(
                att_v.at[head, chunk, 1 - c],
                att_r.at[chunk, :, pl.ds(feats + head * HEAD, HEAD)],
                swap_s, swap_r.at[head], opposite(1 - c),
            )
            return carry

        lax.fori_loop(0, NY, attend, 0)

    left, right = (y + NY - 1) % NY, (y + 1) % NY
    half = rows // 2
    landed(pg.at[left], ag_r.at[0])
    send(pg.at[left, pl.ds(0, half)], pg.at[left, pl.ds(0, half)], ag_s.at[2], ag_r.at[2], at_y(1))
    landed(pg.at[right], ag_r.at[1])
    send(pg.at[right, pl.ds(half, half)], pg.at[right, pl.ds(half, half)], ag_s.at[3], ag_r.at[3], at_y(NY - 1))

    landed(w_v.at[pl.ds(0, feats), :], local_sem.at[3])
    landed(w_v.at[pl.ds(0, feats), :], w_r)
    for head in range(HEADS_HERE):
        landed(att_r.at[:, :, pl.ds(0, 2 * HEAD)], swap_r.at[head])

    def project(tile, carry):
        cols = pl.ds(pl.multiple_of(tile * 256, 256), 256)
        part[:, :, cols] = jnp.dot(
            att_r[...].reshape(NY * rows, 2 * feats), w_v[:, cols], preferred_element_type=F32
        ).reshape(NY, rows, 256)
        return carry

    lax.fori_loop(0, width // 256, project, 0)

    far = (y + 2) % NY
    landed(pg.at[far, pl.ds(0, half)], ag_r.at[2])
    landed(pg.at[far, pl.ds(0, half)], ag_r.at[3])

    group = width // 4
    first_column = (0, 2 * group, group, 3 * group)

    def y_step(k):
        for ch in range(4):
            up = ch % 2 == 0
            block = (y + 2 * NY - 1 - k) % NY if up else (y + 1 + k) % NY
            cols = pl.ds(first_column[ch], group)
            value = part[block, :, cols]
            if k > 0:
                landed(rs_r.at[ch, k - 1], y_r.at[ch, k - 1])
                value = value + rs_r[ch, k - 1].astype(F32)
            if k < NY - 1:
                rs_s[ch, k] = value.astype(BF)
                send(
                    rs_s.at[ch, k], rs_r.at[ch, k], y_s.at[ch, k], y_r.at[ch, k], at_y(1 if up else NY - 1)
                )
            else:
                gated_out[:, cols] = (gate[:, cols] * value).astype(BF)
                gg[q, :, cols] = jnp.sum(grad_v[:, cols].astype(F32) * value, axis=0, keepdims=True)

    y_step(0)

    zcols = width // NZ
    xcols = zcols // NX

    def wgrad(i, carry):
        sign = 2 * (i % 2) - 1
        block = (z + NZ + sign * (i // 2 + 1) * (1 - i // 7)) % NZ
        cols = pl.ds(pl.multiple_of(block * zcols, HEAD), zcols)
        product = lax.dot_general(
            pg[:, :, cols].reshape(NY * rows, zcols),
            att_r[...].reshape(NY * rows, 2 * feats),
            (((0,), (0,)), ((), ())),
            preferred_element_type=F32,
        )
        own[block] = product[:, :feats].reshape(NX, xcols, feats)
        ex_s[block] = product[:, feats:].astype(BF).reshape(NX, xcols, feats)
        send(ex_s.at[block], ex_r.at[block], ex_ss, ex_rs.at[i], other)
        return carry

    def exchanged(i):
        landed(ex_r.at[0], ex_rs.at[i])

    z_chains = ((2, 1), (3, -1), (1, 1), (0, -1))

    def z_step(k):
        if k < 4:
            exchanged(2 * k)
            exchanged(2 * k + 1)
        for ch, (j, way) in enumerate(z_chains):
            xb = (x + j) % NX
            block = (z + 2 * NZ - way * (1 + k)) % NZ
            value = own[block, xb] + ex_r[block, xb].astype(F32)
            if k > 0:
                landed(zr.at[ch, k - 1], z_r.at[ch, k - 1])
                value = value + zr[ch, k - 1].astype(F32)
            if k < NZ - 1:
                zs[ch, k] = value.astype(BF)
                send(
                    zs.at[ch, k], zr.at[ch, k], z_s.at[ch, k], z_r.at[ch, k], at_z(1 if way > 0 else NZ - 1)
                )
            elif j > 0:
                xs[j - 1] = value.astype(BF)
                send(xs.at[j - 1], xr.at[j - 1], x_s.at[j - 1], x_r.at[j - 1], at_x(j))
            else:
                xown[...] = value

    lax.fori_loop(0, 4, wgrad, 0)
    z_step(0)
    lax.fori_loop(4, 8, wgrad, 0)
    z_step(1)
    y_step(1)
    z_step(2)
    z_step(3)
    y_step(2)
    z_step(4)
    z_step(5)
    y_step(3)

    def gate_sums(k, carry):
        send(gg.at[q], gg.at[q], gg_s, gg_r, at_seq((q + k) % NQ))
        return carry

    lax.fori_loop(1, NQ, gate_sums, 0)
    z_step(6)
    z_step(7)

    landed(gg.at[pl.ds(0, NQ - 1)], gg_r)
    total = gg[0]
    for k in range(1, NQ):
        total = total + gg[k]
    ggrad_out[...] = total

    value = xown[...]
    for j in range(NX - 1):
        landed(xr.at[j], x_r.at[j])
        value = value + xr[j].astype(F32)
    wgrad_out[...] = value

    landed(qkv_v.at[:, :, pl.ds(0, (NQ - 1) * rows), :], a2a_s)
    landed(att_v, swap_s)
    landed(w_v.at[pl.ds(0, feats), :], w_s)
    for k in range(2):
        landed(pg.at[0], ag_s.at[k])
        landed(pg.at[0, pl.ds(0, half)], ag_s.at[2 + k])
    for ch in range(4):
        for k in range(NY - 1):
            landed(rs_s.at[ch, k], y_s.at[ch, k])
        for k in range(NZ - 1):
            landed(zs.at[ch, k], z_s.at[ch, k])
    landed(gg.at[pl.ds(0, NQ - 1)], gg_s)
    landed(ex_s, ex_ss)
    for j in range(NX - 1):
        landed(xs.at[j], x_s.at[j])


def per_device(qkv_rows, gate, out_weight, out_grad, tile_order, window):
    rows, wide = qkv_rows.shape[2:]
    width = out_grad.shape[3]
    feats = HEADS_HERE * HEAD
    tokens = rows * NQ
    zcols = width // NZ
    xcols = zcols // NX
    group = width // 4
    vmem = pl.BlockSpec(memory_space=pltpu.VMEM)
    anywhere = pl.BlockSpec(memory_space=pl.ANY)
    dma = pltpu.SemaphoreType.DMA
    scratch = [
        pltpu.VMEM((HEADS_HERE, 3, tokens, HEAD), BF),
        pltpu.VMEM((tokens, HEAD), BF),
        pltpu.VMEM((tokens, HEAD), BF),
        pltpu.VMEM((HEADS_HERE, NY, 2, rows, HEAD), BF),
        pltpu.VMEM((NY, rows, 2 * feats), BF),
        pltpu.VMEM((2 * feats, width), BF),
        pltpu.VMEM((rows, width), BF),
        pltpu.VMEM((NY, rows, width), BF),
        pltpu.VMEM((NY, rows, width), F32),
        pltpu.VMEM((4, NY - 1, rows, group), BF),
        pltpu.VMEM((4, NY - 1, rows, group), BF),
        pltpu.VMEM((NQ, 1, width), F32),
        pltpu.VMEM((NZ, NX, xcols, feats), F32),
        pltpu.VMEM((NZ, NX, xcols, feats), BF),
        pltpu.VMEM((NZ, NX, xcols, feats), BF),
        pltpu.VMEM((4, NZ - 1, xcols, feats), BF),
        pltpu.VMEM((4, NZ - 1, xcols, feats), BF),
        pltpu.VMEM((NX - 1, xcols, feats), BF),
        pltpu.VMEM((NX - 1, xcols, feats), BF),
        pltpu.VMEM((xcols, feats), F32),
        dma((5,)), dma(()), dma((HEADS_HERE,)), dma(()), dma((HEADS_HERE,)), dma(()), dma(()),
        dma((4,)), dma((4,)), dma((4, NY - 1)), dma((4, NY - 1)), dma(()), dma(()), dma(()), dma((NZ,)),
        dma((4, NZ - 1)), dma((4, NZ - 1)), dma((NX - 1,)), dma((NX - 1,)),
    ]
    gated_out, wgrad, ggrad = pl.pallas_call(
        kernel,
        out_shape=(
            jax.ShapeDtypeStruct((rows, width), BF),
            jax.ShapeDtypeStruct((xcols, feats), F32),
            jax.ShapeDtypeStruct((1, width), F32),
        ),
        in_specs=[anywhere, vmem, anywhere, anywhere, vmem, vmem],
        out_specs=(vmem, vmem, vmem),
        scratch_shapes=scratch,
        compiler_params=pltpu.CompilerParams(
            collective_id=0, has_side_effects=True, vmem_limit_bytes=56 * 2**20
        ),
    )(
        qkv_rows.reshape(rows, wide),
        gate.reshape(1, width),
        out_weight,
        out_grad.reshape(rows, width),
        tile_order.reshape(1, tokens),
        window,
    )
    return (
        gated_out.reshape(1, 1, rows, width),
        wgrad.T,
        ggrad.reshape(1, 1, width),
    )


def solution(mesh):
    placed = (
        P("section", "dp", "seq", None),
        P("section", "dp", None),
        P("seq", None),
        P("section", "dp", "seq", None),
        P(),
        P(),
    )
    return jax.shard_map(
        per_device,
        mesh=mesh,
        in_specs=placed,
        out_specs=(
            P("section", "dp", "seq", None),
            P("seq", ("section", "dp")),
            P("section", "dp", None),
        ),
        check_vma=False,
    )
```

```python
import functools
import math

import jax
import jax.numpy as jnp
from jax import lax
from jax.experimental import pallas as pl
from jax.experimental.pallas import tpu as pltpu
from jax.sharding import PartitionSpec as P

MESH = pl.DeviceIdType.MESH
TILE = 64
HEAD = 128
BF = jnp.bfloat16
F32 = jnp.float32
MASKED = -(2.0**30)
NY, NX, NZ, NQ = 4, 4, 8, 8
HEADS_HERE = 3


def kernel(
    qkv, gate, weight, grad, order, window,
    gated_out, wgrad_out, ggrad_out,
    qkv_v, qx, kx, att_v, att_r, w_v, grad_v, pg, part, rs_s, rs_r, gg,
    own, ex_s, ex_r, zs, zr, xs, xr, xown,
    local_sem, a2a_s, a2a_r, swap_s, swap_r, w_s, w_r, ag_s, ag_r, y_s, y_r,
    gg_s, gg_r, ex_ss, ex_rs, z_s, z_r, x_s, x_r,
):
    sec, dp, q = lax.axis_index("section"), lax.axis_index("dp"), lax.axis_index("seq")
    zl, x = dp // NX, dp % NX
    y, c = q // 2, q % 2
    z = sec * (NZ // 2) + zl
    rows = qkv.shape[0]
    width = grad.shape[1]
    feats = HEADS_HERE * HEAD

    def at_seq(j):
        return {"seq": j}

    def at_y(dy):
        return {"seq": ((y + dy) % NY) * 2 + c}

    def at_z(dz):
        there = (z + dz) % NZ
        return {"section": there // (NZ // 2), "dp": (there % (NZ // 2)) * NX + x}

    def at_x(dx):
        return {"dp": zl * NX + (x + dx) % NX}

    def opposite(core):
        return {"section": 1 - sec, "seq": y * 2 + core}

    other = {"seq": y * 2 + 1 - c}

    def send(src, dst, s_sem, r_sem, where):
        copy = pltpu.make_async_remote_copy(
            src_ref=src, dst_ref=dst, send_sem=s_sem, recv_sem=r_sem, device_id=where, device_id_type=MESH
        )
        copy.start()

    def landed(ref, sem):
        pltpu.make_async_copy(ref, ref, sem).wait()

    barrier = pltpu.get_barrier_semaphore()
    partners = [at_seq((q + k) % NQ) for k in range(1, NQ)]
    partners += [opposite(0), opposite(1), at_z(1), at_z(NZ - 1)]
    partners += [at_x(k) for k in range(1, NX)]
    for partner in partners:
        pl.semaphore_signal(barrier, inc=1, device_id=partner, device_id_type=MESH)
    pl.semaphore_wait(barrier, len(partners))

    mine = pl.ds(pl.multiple_of(q * rows, rows), rows)
    for head in range(HEADS_HERE):
        for what in range(3):

            def columns(j):
                return pl.ds(pl.multiple_of(what * width + j * feats + head * HEAD, HEAD), HEAD)

            def one_peer(k, carry):
                j = (q + k) % NQ
                send(
                    qkv.at[:, columns(j)], qkv_v.at[head, what, mine, :], a2a_s, a2a_r.at[head], at_seq(j)
                )
                return carry

            lax.fori_loop(1, NQ, one_peer, 0)
            pltpu.make_async_copy(
                qkv.at[:, columns(q)], qkv_v.at[head, what, mine, :], local_sem.at[head]
            ).start()

    send(weight, w_v.at[pl.ds(feats, feats), :], w_s, w_r, other)
    pltpu.make_async_copy(weight, w_v.at[pl.ds(0, feats), :], local_sem.at[3]).start()
    pltpu.make_async_copy(grad, grad_v, local_sem.at[4]).start()

    slot_tile = lax.broadcasted_iota(jnp.int32, (NQ * rows, HEAD), 0) >> 6
    in_tile = jnp.where(slot_tile == lax.broadcasted_iota(jnp.int32, (NQ * rows, HEAD), 1), 1.0, 0.0).astype(BF)
    tiles = window.shape[1]
    tile_ids = lax.broadcasted_iota(jnp.int32, (HEAD, tiles), 0)
    chosen = tile_ids == window[0:1, :]
    for k in range(1, window.shape[0]):
        chosen = jnp.logical_or(chosen, tile_ids == window[k : k + 1, :])
    bias = jnp.where(chosen, 0.0, MASKED)
    bias = jnp.concatenate([bias, jnp.zeros((HEAD, HEAD - tiles), F32)], axis=1).astype(BF)
    for part_of in range(NY):
        here = pl.ds(part_of * 2 * rows, 2 * rows)
        tokens = lax.broadcasted_iota(jnp.int32, (2 * rows, NQ * rows), 0) + part_of * 2 * rows
        placed = jnp.where(tokens == order[...], 1.0, 0.0).astype(BF)
        tile_of = jnp.dot(placed, in_tile, preferred_element_type=F32).astype(BF)
        kx[here, :] = tile_of
        qx[here, :] = lax.dot_general(
            tile_of, bias, (((1,), (1,)), ((), ())), preferred_element_type=F32
        ).astype(BF)

    pltpu.make_async_copy(grad, grad_v, local_sem.at[4]).wait()

    def block_at(i):
        sign = 2 * (i % 2) - 1
        return (z + NZ + sign * (i // 2 + 1) * (1 - i // 7)) % NZ

    zcols = width // NZ
    xcols = zcols // NX

    def cotangent(i, carry):
        cols = pl.ds(pl.multiple_of(block_at(i) * zcols, HEAD), zcols)
        pg[i, y] = (gate[:, cols] * grad_v[:, cols].astype(F32)).astype(BF)
        return carry

    lax.fori_loop(0, NZ, cotangent, 0)

    left, right, far = (y + NY - 1) % NY, (y + 1) % NY, (y + 2) % NY
    half = rows // 2

    def spread(m):
        own_rows = pg.at[pl.ds(2 * m, 2), y]
        send(own_rows, own_rows, ag_s.at[0, m], ag_r.at[0, m], at_y(1))
        send(own_rows, own_rows, ag_s.at[1, m], ag_r.at[1, m], at_y(NY - 1))

    def pass_on(m):
        two = pl.ds(2 * m, 2)
        landed(pg.at[two, left], ag_r.at[0, m])
        upper = pg.at[two, left, pl.ds(0, half)]
        send(upper, upper, ag_s.at[2, m], ag_r.at[2, m], at_y(1))
        landed(pg.at[two, right], ag_r.at[1, m])
        lower = pg.at[two, right, pl.ds(half, half)]
        send(lower, lower, ag_s.at[3, m], ag_r.at[3, m], at_y(NY - 1))

    def spread_done(m):
        landed(pg.at[pl.ds(2 * m, 2), far, pl.ds(0, half)], ag_r.at[2, m])
        landed(pg.at[pl.ds(2 * m, 2), far, pl.ds(half, half)], ag_r.at[3, m])

    scale = 1.0 / math.sqrt(HEAD)
    for head in range(HEADS_HERE):
        landed(qkv_v.at[head, :, pl.ds(0, (NQ - 1) * rows), :], a2a_r.at[head])
        landed(qkv_v.at[head, :, pl.ds(0, rows), :], local_sem.at[head])
        if head == HEADS_HERE - 1:
            spread(0)
            spread(1)

        def attend(chunk, carry):
            here = pl.ds(pl.multiple_of(chunk * 2 * rows, 2 * rows), 2 * rows)
            queries = jnp.concatenate([qkv_v[head, 0, here, :], qx[here, :]], axis=1)
            keys = jnp.concatenate([qkv_v[head, 1], kx[...]], axis=1)
            scores = lax.dot_general(
                queries, keys, (((1,), (1,)), ((), ())), preferred_element_type=F32
            )
            top = jnp.max(scores, axis=1, keepdims=True)
            powers = jnp.exp((scores - top) * scale)
            total = jnp.sum(powers, axis=1, keepdims=True)
            mixed = jnp.dot(powers.astype(BF), qkv_v[head, 2], preferred_element_type=F32) / total
            att_v[head, chunk] = mixed.astype(BF).reshape(2, rows, HEAD)
            send(
                att_v.at[head, chunk, c],
                att_r.at[chunk, :, pl.ds(head * HEAD, HEAD)],
                swap_s, swap_r.at[head], opposite(c),
            )
            send(
                att_v.at[head, chunk, 1 - c],
                att_r.at[chunk, :, pl.ds(feats + head * HEAD, HEAD)],
                swap_s, swap_r.at[head], opposite(1 - c),
            )
            return carry

        lax.fori_loop(0, NY, attend, 0)

    pass_on(0)
    spread(2)
    pass_on(1)
    spread(3)
    pass_on(2)
    pass_on(3)

    landed(w_v.at[pl.ds(0, feats), :], local_sem.at[3])
    landed(w_v.at[pl.ds(0, feats), :], w_r)
    for head in range(HEADS_HERE):
        landed(att_r.at[:, :, pl.ds(0, 2 * HEAD)], swap_r.at[head])

    def project(i, carry):
        tile = 3 * (i // 3 % 2 * 2 + i // 6) + i % 3
        cols = pl.ds(pl.multiple_of(tile * 256, 256), 256)
        part[:, :, cols] = jnp.dot(
            att_r[...].reshape(NY * rows, 2 * feats), w_v[:, cols], preferred_element_type=F32
        ).reshape(NY, rows, 256)
        return carry

    group = width // 4
    first_column = (0, 2 * group, group, 3 * group)

    def y_step(k, pair):
        for ch in (2 * pair, 2 * pair + 1):
            up = ch % 2 == 0
            block = (y + 2 * NY - 1 - k) % NY if up else (y + 1 + k) % NY
            cols = pl.ds(first_column[ch], group)
            value = part[block, :, cols]
            if k > 0:
                landed(rs_r.at[ch, k - 1], y_r.at[ch, k - 1])
                value = value + rs_r[ch, k - 1].astype(F32)
            if k < NY - 1:
                rs_s[ch, k] = value.astype(BF)
                send(
                    rs_s.at[ch, k], rs_r.at[ch, k], y_s.at[ch, k], y_r.at[ch, k], at_y(1 if up else NY - 1)
                )
            else:
                gated_out[:, cols] = (gate[:, cols] * value).astype(BF)
                gg[pair, q, :, pl.ds(ch % 2 * group, group)] = jnp.sum(
                    grad_v[:, cols].astype(F32) * value, axis=0, keepdims=True
                )

    def wgrad(i, carry):
        block = block_at(i)
        product = lax.dot_general(
            pg[i].reshape(NY * rows, zcols),
            att_r[...].reshape(NY * rows, 2 * feats),
            (((0,), (0,)), ((), ())),
            preferred_element_type=F32,
        )
        own[block] = product[:, :feats].reshape(NX, xcols, feats)
        ex_s[block] = product[:, feats:].astype(BF).reshape(NX, xcols, feats)
        send(ex_s.at[block], ex_r.at[block], ex_ss, ex_rs.at[i], other)
        return carry

    def exchanged(i):
        landed(ex_r.at[0], ex_rs.at[i])

    z_chains = ((2, 1), (3, -1), (1, 1), (0, -1))

    def z_step(k):
        if k < 4:
            exchanged(2 * k)
            exchanged(2 * k + 1)
        for ch, (j, way) in enumerate(z_chains):
            xb = (x + j) % NX
            block = (z + 2 * NZ - way * (1 + k)) % NZ
            value = own[block, xb] + ex_r[block, xb].astype(F32)
            if k > 0:
                landed(zr.at[ch, k - 1], z_r.at[ch, k - 1])
                value = value + zr[ch, k - 1].astype(F32)
            if k < NZ - 1:
                zs[ch, k] = value.astype(BF)
                send(
                    zs.at[ch, k], zr.at[ch, k], z_s.at[ch, k], z_r.at[ch, k], at_z(1 if way > 0 else NZ - 1)
                )
            elif j > 0:
                xs[j - 1] = value.astype(BF)
                send(xs.at[j - 1], xr.at[j - 1], x_s.at[j - 1], x_r.at[j - 1], at_x(j))
            else:
                xown[...] = value

    def gate_sums(pair):
        def one_peer(k, carry):
            send(gg.at[pair, q], gg.at[pair, q], gg_s, gg_r.at[pair], at_seq((q + k) % NQ))
            return carry

        lax.fori_loop(1, NQ, one_peer, 0)

    def project_pair(pair):
        lax.fori_loop(6 * pair, 6 * pair + 6, project, 0)

    spread_done(0)
    lax.fori_loop(0, 2, wgrad, 0)
    spread_done(1)
    lax.fori_loop(2, 4, wgrad, 0)
    z_step(0)
    project_pair(0)
    y_step(0, 0)
    z_step(1)
    project_pair(1)
    y_step(0, 1)
    spread_done(2)
    lax.fori_loop(4, 6, wgrad, 0)
    spread_done(3)
    lax.fori_loop(6, 8, wgrad, 0)
    z_step(2)
    y_step(1, 0)
    z_step(3)
    y_step(1, 1)
    z_step(4)
    z_step(5)
    y_step(2, 0)
    z_step(6)
    y_step(2, 1)
    z_step(7)
    y_step(3, 0)
    gate_sums(0)
    y_step(3, 1)
    gate_sums(1)

    value = xown[...]
    for j in range(NX - 1):
        landed(xr.at[j], x_r.at[j])
        value = value + xr[j].astype(F32)
    wgrad_out[...] = value

    for pair in range(2):
        landed(gg.at[0, pl.ds(0, NQ - 1)], gg_r.at[pair])
        total = gg[pair, 0]
        for k in range(1, NQ):
            total = total + gg[pair, k]
        for side in range(2):
            ggrad_out[:, pl.ds(first_column[2 * pair + side], group)] = total[:, side * group : (side + 1) * group]

    landed(qkv_v.at[:, :, pl.ds(0, (NQ - 1) * rows), :], a2a_s)
    landed(att_v, swap_s)
    landed(w_v.at[pl.ds(0, feats), :], w_s)
    for m in range(NZ // 2):
        for k in range(2):
            landed(pg.at[pl.ds(0, 2), 0], ag_s.at[k, m])
            landed(pg.at[pl.ds(0, 2), 0, pl.ds(0, half)], ag_s.at[2 + k, m])
    for ch in range(4):
        for k in range(NY - 1):
            landed(rs_s.at[ch, k], y_s.at[ch, k])
        for k in range(NZ - 1):
            landed(zs.at[ch, k], z_s.at[ch, k])
    landed(gg.at[:, pl.ds(0, NQ - 1)], gg_s)
    landed(ex_s, ex_ss)
    for j in range(NX - 1):
        landed(xs.at[j], x_s.at[j])


def finish(gated, wgrad, ggrad, gated_out, wgrad_out, ggrad_out):
    gated_out[...] = gated[...]
    ggrad_out[...] = ggrad[...]
    wgrad_out[...] = wgrad[...]


def per_device(qkv_rows, gate, out_weight, out_grad, tile_order, window):
    rows, wide = qkv_rows.shape[2:]
    width = out_grad.shape[3]
    feats = HEADS_HERE * HEAD
    tokens = rows * NQ
    zcols = width // NZ
    xcols = zcols // NX
    group = width // 4
    vmem = pl.BlockSpec(memory_space=pltpu.VMEM)
    anywhere = pl.BlockSpec(memory_space=pl.ANY)
    dma = pltpu.SemaphoreType.DMA
    scratch = [
        pltpu.VMEM((HEADS_HERE, 3, tokens, HEAD), BF),
        pltpu.VMEM((tokens, HEAD), BF),
        pltpu.VMEM((tokens, HEAD), BF),
        pltpu.VMEM((HEADS_HERE, NY, 2, rows, HEAD), BF),
        pltpu.VMEM((NY, rows, 2 * feats), BF),
        pltpu.VMEM((2 * feats, width), BF),
        pltpu.VMEM((rows, width), BF),
        pltpu.VMEM((NZ, NY, rows, zcols), BF),
        pltpu.VMEM((NY, rows, width), F32),
        pltpu.VMEM((4, NY - 1, rows, group), BF),
        pltpu.VMEM((4, NY - 1, rows, group), BF),
        pltpu.VMEM((2, NQ, 1, width // 2), F32),
        pltpu.VMEM((NZ, NX, xcols, feats), F32),
        pltpu.VMEM((NZ, NX, xcols, feats), BF),
        pltpu.VMEM((NZ, NX, xcols, feats), BF),
        pltpu.VMEM((4, NZ - 1, xcols, feats), BF),
        pltpu.VMEM((4, NZ - 1, xcols, feats), BF),
        pltpu.VMEM((NX - 1, xcols, feats), BF),
        pltpu.VMEM((NX - 1, xcols, feats), BF),
        pltpu.VMEM((xcols, feats), F32),
        dma((5,)), dma(()), dma((HEADS_HERE,)), dma(()), dma((HEADS_HERE,)), dma(()), dma(()),
        dma((4, NZ // 2)), dma((4, NZ // 2)), dma((4, NY - 1)), dma((4, NY - 1)), dma(()), dma((2,)), dma(()), dma((NZ,)),
        dma((4, NZ - 1)), dma((4, NZ - 1)), dma((NX - 1,)), dma((NX - 1,)),
    ]
    gated_out, wgrad, ggrad = pl.pallas_call(
        kernel,
        out_shape=(
            jax.ShapeDtypeStruct((rows, width), BF),
            jax.ShapeDtypeStruct((xcols, feats), F32),
            jax.ShapeDtypeStruct((1, width), F32),
        ),
        in_specs=[anywhere, vmem, anywhere, anywhere, vmem, vmem],
        out_specs=(vmem, vmem, vmem),
        scratch_shapes=scratch,
        compiler_params=pltpu.CompilerParams(
            collective_id=0, has_side_effects=True, vmem_limit_bytes=56 * 2**20
        ),
    )(
        qkv_rows.reshape(rows, wide),
        gate.reshape(1, width),
        out_weight,
        out_grad.reshape(rows, width),
        tile_order.reshape(1, tokens),
        window.T,
    )
    gated_out, wgrad, ggrad = pl.pallas_call(
        finish,
        out_shape=(
            jax.ShapeDtypeStruct((rows, width), BF),
            jax.ShapeDtypeStruct((xcols, feats), F32),
            jax.ShapeDtypeStruct((1, width), F32),
        ),
        in_specs=[vmem, vmem, vmem],
        out_specs=(vmem, vmem, vmem),
    )(gated_out, wgrad, ggrad)
    return (
        gated_out.reshape(1, 1, rows, width),
        wgrad.T,
        ggrad.reshape(1, 1, width),
    )


def solution(mesh):
    placed = (
        P("section", "dp", "seq", None),
        P("section", "dp", None),
        P("seq", None),
        P("section", "dp", "seq", None),
        P(),
        P(),
    )
    return jax.shard_map(
        per_device,
        mesh=mesh,
        in_specs=placed,
        out_specs=(
            P("section", "dp", "seq", None),
            P("seq", ("section", "dp")),
            P("section", "dp", None),
        ),
        check_vma=False,
    )
```

```python
import functools
import math

import jax
import jax.numpy as jnp
from jax import lax
from jax.experimental import pallas as pl
from jax.experimental.pallas import tpu as pltpu
from jax.sharding import PartitionSpec as P

MESH = pl.DeviceIdType.MESH
TILE = 64
HEAD = 128
BF = jnp.bfloat16
F32 = jnp.float32
MASKED = -(2.0**30)
NY, NX, NZ, NQ = 4, 4, 8, 8
HEADS_HERE = 3


def kernel(
    qkv, gate, weight, grad, order, window,
    gated_out, wgrad_out, ggrad_out,
    qkv_v, qx, kx, att_v, att_r, w_v, grad_v, pg, part, rs_s, rs_r, gg,
    own, ex_s, ex_r, zs, zr, xs, xr, xown,
    local_sem, a2a_s, a2a_r, swap_s, swap_r, w_s, w_r, ag_s, ag_r, y_s, y_r,
    gg_s, gg_r, ex_ss, ex_rs, z_s, z_r, x_s, x_r,
):
    sec, dp, q = lax.axis_index("section"), lax.axis_index("dp"), lax.axis_index("seq")
    zl, x = dp // NX, dp % NX
    y, c = q // 2, q % 2
    z = sec * (NZ // 2) + zl
    rows = qkv.shape[0]
    width = grad.shape[1]
    feats = HEADS_HERE * HEAD

    def at_seq(j):
        return {"seq": j}

    def at_y(dy):
        return {"seq": ((y + dy) % NY) * 2 + c}

    def at_z(dz):
        there = (z + dz) % NZ
        return {"section": there // (NZ // 2), "dp": (there % (NZ // 2)) * NX + x}

    def at_x(dx):
        return {"dp": zl * NX + (x + dx) % NX}

    def opposite(core):
        return {"section": 1 - sec, "seq": y * 2 + core}

    other = {"seq": y * 2 + 1 - c}

    def send(src, dst, s_sem, r_sem, where):
        copy = pltpu.make_async_remote_copy(
            src_ref=src, dst_ref=dst, send_sem=s_sem, recv_sem=r_sem, device_id=where, device_id_type=MESH
        )
        copy.start()

    def landed(ref, sem):
        pltpu.make_async_copy(ref, ref, sem).wait()

    barrier = pltpu.get_barrier_semaphore()
    partners = [at_seq((q + k) % NQ) for k in range(1, NQ)]
    partners += [opposite(0), opposite(1), at_z(1), at_z(NZ - 1)]
    partners += [at_x(k) for k in range(1, NX)]
    for partner in partners:
        pl.semaphore_signal(barrier, inc=1, device_id=partner, device_id_type=MESH)
    pl.semaphore_wait(barrier, len(partners))

    mine = pl.ds(pl.multiple_of(q * rows, rows), rows)
    for head in range(HEADS_HERE):
        for what in range(3):

            def columns(j):
                return pl.ds(pl.multiple_of(what * width + j * feats + head * HEAD, HEAD), HEAD)

            def one_peer(k, carry):
                j = (q + k) % NQ
                send(
                    qkv.at[:, columns(j)], qkv_v.at[head, what, mine, :], a2a_s, a2a_r.at[head], at_seq(j)
                )
                return carry

            lax.fori_loop(1, NQ, one_peer, 0)
            pltpu.make_async_copy(
                qkv.at[:, columns(q)], qkv_v.at[head, what, mine, :], local_sem.at[head]
            ).start()

    send(weight, w_v.at[pl.ds(feats, feats), :], w_s, w_r, other)
    pltpu.make_async_copy(weight, w_v.at[pl.ds(0, feats), :], local_sem.at[3]).start()
    pltpu.make_async_copy(grad, grad_v, local_sem.at[4]).start()

    slot_tile = lax.broadcasted_iota(jnp.int32, (NQ * rows, HEAD), 0) >> 6
    in_tile = jnp.where(slot_tile == lax.broadcasted_iota(jnp.int32, (NQ * rows, HEAD), 1), 1.0, 0.0).astype(BF)
    tiles = window.shape[1]
    tile_ids = lax.broadcasted_iota(jnp.int32, (HEAD, tiles), 0)
    chosen = tile_ids == window[0:1, :]
    for k in range(1, window.shape[0]):
        chosen = jnp.logical_or(chosen, tile_ids == window[k : k + 1, :])
    bias = jnp.where(chosen, 0.0, MASKED)
    bias = jnp.concatenate([bias, jnp.zeros((HEAD, HEAD - tiles), F32)], axis=1).astype(BF)
    for part_of in range(NY):
        here = pl.ds(part_of * 2 * rows, 2 * rows)
        tokens = lax.broadcasted_iota(jnp.int32, (2 * rows, NQ * rows), 0) + part_of * 2 * rows
        placed = jnp.where(tokens == order[...], 1.0, 0.0).astype(BF)
        tile_of = jnp.dot(placed, in_tile, preferred_element_type=F32).astype(BF)
        kx[here, :] = tile_of
        qx[here, :] = lax.dot_general(
            tile_of, bias, (((1,), (1,)), ((), ())), preferred_element_type=F32
        ).astype(BF)

    pltpu.make_async_copy(grad, grad_v, local_sem.at[4]).wait()

    def block_at(i):
        return (z + NZ + (1 - 2 * (i % 2)) * (NZ // 2 - (i + 1) // 2)) % NZ

    zcols = width // NZ
    xcols = zcols // NX

    def cotangent(i, carry):
        cols = pl.ds(pl.multiple_of(block_at(i) * zcols, HEAD), zcols)
        pg[i, y] = (gate[:, cols] * grad_v[:, cols].astype(F32)).astype(BF)
        return carry

    lax.fori_loop(0, NZ, cotangent, 0)

    left, right, far = (y + NY - 1) % NY, (y + 1) % NY, (y + 2) % NY
    half = rows // 2

    def spread(m):
        own_rows = pg.at[pl.ds(2 * m, 2), y]
        send(own_rows, own_rows, ag_s.at[0, m], ag_r.at[0, m], at_y(1))
        send(own_rows, own_rows, ag_s.at[1, m], ag_r.at[1, m], at_y(NY - 1))

    def pass_on(m):
        two = pl.ds(2 * m, 2)
        landed(pg.at[two, left], ag_r.at[0, m])
        upper = pg.at[two, left, pl.ds(0, half)]
        send(upper, upper, ag_s.at[2, m], ag_r.at[2, m], at_y(1))
        landed(pg.at[two, right], ag_r.at[1, m])
        lower = pg.at[two, right, pl.ds(half, half)]
        send(lower, lower, ag_s.at[3, m], ag_r.at[3, m], at_y(NY - 1))

    def spread_done(m):
        landed(pg.at[pl.ds(2 * m, 2), far, pl.ds(0, half)], ag_r.at[2, m])
        landed(pg.at[pl.ds(2 * m, 2), far, pl.ds(half, half)], ag_r.at[3, m])

    scale = 1.0 / math.sqrt(HEAD)
    for head in range(HEADS_HERE):
        if head == HEADS_HERE - 1:
            for m in range(NZ // 2):
                spread(m)
        landed(qkv_v.at[head, :, pl.ds(0, (NQ - 1) * rows), :], a2a_r.at[head])
        landed(qkv_v.at[head, :, pl.ds(0, rows), :], local_sem.at[head])

        def attend(chunk, carry):
            here = pl.ds(pl.multiple_of(chunk * 2 * rows, 2 * rows), 2 * rows)
            queries = jnp.concatenate([qkv_v[head, 0, here, :], qx[here, :]], axis=1)
            keys = jnp.concatenate([qkv_v[head, 1], kx[...]], axis=1)
            scores = lax.dot_general(
                queries, keys, (((1,), (1,)), ((), ())), preferred_element_type=F32
            )
            top = jnp.max(scores, axis=1, keepdims=True)
            powers = jnp.exp((scores - top) * scale)
            total = jnp.sum(powers, axis=1, keepdims=True)
            mixed = jnp.dot(powers.astype(BF), qkv_v[head, 2], preferred_element_type=F32) / total
            att_v[head, chunk] = mixed.astype(BF).reshape(2, rows, HEAD)
            send(
                att_v.at[head, chunk, c],
                att_r.at[chunk, :, pl.ds(head * HEAD, HEAD)],
                swap_s, swap_r.at[head], opposite(c),
            )
            send(
                att_v.at[head, chunk, 1 - c],
                att_r.at[chunk, :, pl.ds(feats + head * HEAD, HEAD)],
                swap_s, swap_r.at[head], opposite(1 - c),
            )
            return carry

        lax.fori_loop(0, NY, attend, 0)

    pass_on(0)
    pass_on(1)
    pass_on(2)
    pass_on(3)

    landed(w_v.at[pl.ds(0, feats), :], local_sem.at[3])
    landed(w_v.at[pl.ds(0, feats), :], w_r)
    for head in range(HEADS_HERE):
        landed(att_r.at[:, :, pl.ds(0, 2 * HEAD)], swap_r.at[head])

    def project(i, carry):
        tile = 3 * (i // 3 % 2 * 2 + i // 6) + i % 3
        cols = pl.ds(pl.multiple_of(tile * 256, 256), 256)
        part[:, :, cols] = jnp.dot(
            att_r[...].reshape(NY * rows, 2 * feats), w_v[:, cols], preferred_element_type=F32
        ).reshape(NY, rows, 256)
        return carry

    group = width // 4
    first_column = (0, 2 * group, group, 3 * group)

    def y_step(k, pair):
        for ch in (2 * pair, 2 * pair + 1):
            up = ch % 2 == 0
            block = (y + 2 * NY - 1 - k) % NY if up else (y + 1 + k) % NY
            cols = pl.ds(first_column[ch], group)
            value = part[block, :, cols]
            if k > 0:
                landed(rs_r.at[ch, k - 1], y_r.at[ch, k - 1])
                value = value + rs_r[ch, k - 1].astype(F32)
            if k < NY - 1:
                rs_s[ch, k] = value.astype(BF)
                send(
                    rs_s.at[ch, k], rs_r.at[ch, k], y_s.at[ch, k], y_r.at[ch, k], at_y(1 if up else NY - 1)
                )
            else:
                gated_out[:, cols] = (gate[:, cols] * value).astype(BF)
                gg[pair, q, :, pl.ds(ch % 2 * group, group)] = jnp.sum(
                    grad_v[:, cols].astype(F32) * value, axis=0, keepdims=True
                )

    def wgrad(i, carry):
        block = block_at(i)
        product = lax.dot_general(
            pg[i].reshape(NY * rows, zcols),
            att_r[...].reshape(NY * rows, 2 * feats),
            (((0,), (0,)), ((), ())),
            preferred_element_type=F32,
        )
        own[block] = product[:, :feats].reshape(NX, xcols, feats)
        ex_s[block] = product[:, feats:].astype(BF).reshape(NX, xcols, feats)
        send(ex_s.at[block], ex_r.at[block], ex_ss, ex_rs.at[i], other)
        return carry

    def exchanged(i):
        landed(ex_r.at[0], ex_rs.at[i])

    z_chains = ((2, 1), (3, -1), (1, 1), (0, -1))

    far_hops = NZ // 2

    def z_step(k):
        for i in ((0, 1, 2), (3, 4), (5, 6), (), (7,))[k]:
            exchanged(i)
        for ch, (j, way) in enumerate(z_chains):
            xb = (x + j) % NX
            if k == far_hops:
                value = own[z, xb] + ex_r[z, xb].astype(F32)
                for slot in (far_hops - 1, NZ - 2):
                    landed(zr.at[ch, slot], z_r.at[ch, slot])
                    value = value + zr[ch, slot].astype(F32)
                if j > 0:
                    xs[j - 1] = value.astype(BF)
                    send(xs.at[j - 1], xr.at[j - 1], x_s.at[j - 1], x_r.at[j - 1], at_x(j))
                else:
                    xown[...] = value
                continue
            for hops, first, towards in ((far_hops, 0, way), (far_hops - 1, far_hops, -way)):
                if k >= hops:
                    continue
                block = (z + NZ + towards * (hops - k)) % NZ
                slot = first + k
                value = own[block, xb] + ex_r[block, xb].astype(F32)
                if k > 0:
                    landed(zr.at[ch, slot - 1], z_r.at[ch, slot - 1])
                    value = value + zr[ch, slot - 1].astype(F32)
                zs[ch, slot] = value.astype(BF)
                send(
                    zs.at[ch, slot], zr.at[ch, slot], z_s.at[ch, slot], z_r.at[ch, slot],
                    at_z(1 if towards > 0 else NZ - 1),
                )

    def gate_sums(pair):
        def one_peer(k, carry):
            send(gg.at[pair, q], gg.at[pair, q], gg_s, gg_r.at[pair], at_seq((q + k) % NQ))
            return carry

        lax.fori_loop(1, NQ, one_peer, 0)

    def project_pair(pair):
        lax.fori_loop(6 * pair, 6 * pair + 6, project, 0)

    spread_done(0)
    lax.fori_loop(0, 2, wgrad, 0)
    spread_done(1)
    lax.fori_loop(2, 4, wgrad, 0)
    project_pair(0)
    y_step(0, 0)
    z_step(0)
    project_pair(1)
    y_step(0, 1)
    spread_done(2)
    lax.fori_loop(4, 6, wgrad, 0)
    spread_done(3)
    lax.fori_loop(6, 8, wgrad, 0)
    y_step(1, 0)
    z_step(1)
    y_step(1, 1)
    z_step(2)
    y_step(2, 0)
    y_step(2, 1)
    z_step(3)
    y_step(3, 0)
    gate_sums(0)
    y_step(3, 1)
    gate_sums(1)
    z_step(4)

    value = xown[...]
    for j in range(NX - 1):
        landed(xr.at[j], x_r.at[j])
        value = value + xr[j].astype(F32)
    wgrad_out[...] = value

    for pair in range(2):
        landed(gg.at[0, pl.ds(0, NQ - 1)], gg_r.at[pair])
        total = gg[pair, 0]
        for k in range(1, NQ):
            total = total + gg[pair, k]
        for side in range(2):
            ggrad_out[:, pl.ds(first_column[2 * pair + side], group)] = total[:, side * group : (side + 1) * group]

    landed(qkv_v.at[:, :, pl.ds(0, (NQ - 1) * rows), :], a2a_s)
    landed(att_v, swap_s)
    landed(w_v.at[pl.ds(0, feats), :], w_s)
    for m in range(NZ // 2):
        for k in range(2):
            landed(pg.at[pl.ds(0, 2), 0], ag_s.at[k, m])
            landed(pg.at[pl.ds(0, 2), 0, pl.ds(0, half)], ag_s.at[2 + k, m])
    for ch in range(4):
        for k in range(NY - 1):
            landed(rs_s.at[ch, k], y_s.at[ch, k])
        for k in range(NZ - 1):
            landed(zs.at[ch, k], z_s.at[ch, k])
    landed(gg.at[:, pl.ds(0, NQ - 1)], gg_s)
    landed(ex_s, ex_ss)
    for j in range(NX - 1):
        landed(xs.at[j], x_s.at[j])


def finish(gated, wgrad, ggrad, gated_out, wgrad_out, ggrad_out):
    gated_out[...] = gated[...]
    ggrad_out[...] = ggrad[...]
    wgrad_out[...] = wgrad[...]


def per_device(qkv_rows, gate, out_weight, out_grad, tile_order, window):
    rows, wide = qkv_rows.shape[2:]
    width = out_grad.shape[3]
    feats = HEADS_HERE * HEAD
    tokens = rows * NQ
    zcols = width // NZ
    xcols = zcols // NX
    group = width // 4
    vmem = pl.BlockSpec(memory_space=pltpu.VMEM)
    anywhere = pl.BlockSpec(memory_space=pl.ANY)
    dma = pltpu.SemaphoreType.DMA
    scratch = [
        pltpu.VMEM((HEADS_HERE, 3, tokens, HEAD), BF),
        pltpu.VMEM((tokens, HEAD), BF),
        pltpu.VMEM((tokens, HEAD), BF),
        pltpu.VMEM((HEADS_HERE, NY, 2, rows, HEAD), BF),
        pltpu.VMEM((NY, rows, 2 * feats), BF),
        pltpu.VMEM((2 * feats, width), BF),
        pltpu.VMEM((rows, width), BF),
        pltpu.VMEM((NZ, NY, rows, zcols), BF),
        pltpu.VMEM((NY, rows, width), F32),
        pltpu.VMEM((4, NY - 1, rows, group), BF),
        pltpu.VMEM((4, NY - 1, rows, group), BF),
        pltpu.VMEM((2, NQ, 1, width // 2), F32),
        pltpu.VMEM((NZ, NX, xcols, feats), F32),
        pltpu.VMEM((NZ, NX, xcols, feats), BF),
        pltpu.VMEM((NZ, NX, xcols, feats), BF),
        pltpu.VMEM((4, NZ - 1, xcols, feats), BF),
        pltpu.VMEM((4, NZ - 1, xcols, feats), BF),
        pltpu.VMEM((NX - 1, xcols, feats), BF),
        pltpu.VMEM((NX - 1, xcols, feats), BF),
        pltpu.VMEM((xcols, feats), F32),
        dma((5,)), dma(()), dma((HEADS_HERE,)), dma(()), dma((HEADS_HERE,)), dma(()), dma(()),
        dma((4, NZ // 2)), dma((4, NZ // 2)), dma((4, NY - 1)), dma((4, NY - 1)), dma(()), dma((2,)), dma(()), dma((NZ,)),
        dma((4, NZ - 1)), dma((4, NZ - 1)), dma((NX - 1,)), dma((NX - 1,)),
    ]
    gated_out, wgrad, ggrad = pl.pallas_call(
        kernel,
        out_shape=(
            jax.ShapeDtypeStruct((rows, width), BF),
            jax.ShapeDtypeStruct((xcols, feats), F32),
            jax.ShapeDtypeStruct((1, width), F32),
        ),
        in_specs=[anywhere, vmem, anywhere, anywhere, vmem, vmem],
        out_specs=(vmem, vmem, vmem),
        scratch_shapes=scratch,
        compiler_params=pltpu.CompilerParams(
            collective_id=0, has_side_effects=True, vmem_limit_bytes=56 * 2**20
        ),
    )(
        qkv_rows.reshape(rows, wide),
        gate.reshape(1, width),
        out_weight,
        out_grad.reshape(rows, width),
        tile_order.reshape(1, tokens),
        window.T,
    )
    gated_out, wgrad, ggrad = pl.pallas_call(
        finish,
        out_shape=(
            jax.ShapeDtypeStruct((rows, width), BF),
            jax.ShapeDtypeStruct((xcols, feats), F32),
            jax.ShapeDtypeStruct((1, width), F32),
        ),
        in_specs=[vmem, vmem, vmem],
        out_specs=(vmem, vmem, vmem),
    )(gated_out, wgrad, ggrad)
    return (
        gated_out.reshape(1, 1, rows, width),
        wgrad.T,
        ggrad.reshape(1, 1, width),
    )


def solution(mesh):
    placed = (
        P("section", "dp", "seq", None),
        P("section", "dp", None),
        P("seq", None),
        P("section", "dp", "seq", None),
        P(),
        P(),
    )
    return jax.shard_map(
        per_device,
        mesh=mesh,
        in_specs=placed,
        out_specs=(
            P("section", "dp", "seq", None),
            P("seq", ("section", "dp")),
            P("section", "dp", None),
        ),
        check_vma=False,
    )
```
